128 devices in a mesh: box: 32 (over z, y, core), grp: 4 (over x).
Axes of the slice: x: 4, y: 4, z: 4, core: 2. Of those that a mesh axis runs over, the one named last changes fastest.
Arguments:
- features: bfloat16 [128, 524288], P(None, ('box', 'grp')), may hold values from -6 to 6
- basis_values: bfloat16 [64, 524288], P(None, ('box', 'grp')), may hold values from -6 to 6
- positions: float32 [3, 524288], P(None, ('box', 'grp')), may hold values from 0 to 2
- translation: bfloat16 [2, 316, 64, 64], replicated, may hold values from -0.75 to 0.75
- far_mixing: bfloat16 [2, 128, 128], replicated, may hold values from -0.5 to 0.5
- near_mixing: bfloat16 [2, 128, 128], replicated, may hold values from -0.5 to 0.5
- send_box: int32 [128, 128, 4], P(('box', 'grp')), may hold values from 0 to 63
- source_dev: int32 [8192, 32], P(('box', 'grp')), may hold values from 0 to 127
- source_slot: int32 [8192, 32], P(('box', 'grp')), may hold values from 0 to 3
- offset_class: int32 [8192, 32], P(('box', 'grp')), may hold values from 0 to 315
- near_boxes: int32 [8192, 27], P(('box', 'grp')), may hold values from 0 to 8191, as said below
Outputs:
- updated: bfloat16 [128, 524288], P(None, ('box', 'grp'))
The draws below stay inside these ranges and needn't reach their ends.
Inputs may be any that keep to these rules, and one draw needn't show every extreme that they name: `near_boxes`: the first entry of a box's list is the box itself; every entry lies within 8 boxes of it in the curve order.
All inputs are finite; a program needn't handle non-finite values.
Results may differ from the reference program's by a relative error of at most 0.012.
Values may be sent and summed in bfloat16 or wider, within the bound.
No kernel may reach another device: no remote copies, remote signals or barrier semaphores. Data moves between devices by JAX's collectives and lax.ppermute only.
A program may use at most 192 MiB of HBM per device.

```python
import math
import jax
import jax.numpy as jnp
import numpy as np
from jax import lax

C = 128
K = 64
P_SIZE = 64
BOX_DEV = 64
LAYERS = 2
L_FAR = 32
L_NEAR = 27
NCLASS = 316
CAP = 4
HB = 8
BOXES = 8192
PARTICLES = 524288
DEVICES = 128


def draw_near_boxes(key, part):
    key = jax.random.fold_in(key, 7)
    offsets = jax.random.randint(key, (BOXES, L_NEAR - 1), -HB, HB + 1, dtype=jnp.int32)
    centre = jnp.arange(BOXES, dtype=jnp.int32)[:, None]
    others = jnp.clip(centre + offsets, 0, BOXES - 1)
    return jnp.concatenate([centre, others], axis=1).astype(jnp.int32)


def touch_ends(values, key, low, high):
    shape = values.shape
    spot = [jax.random.randint(jax.random.fold_in(key, axis), (), 0, shape[axis]) for axis in range(len(shape))]
    values = values.at[tuple(spot)].set(low)
    longest = shape.index(max(shape))
    spot[longest] = (spot[longest] + 1) % shape[longest]
    return values.at[tuple(spot)].set(high)


def shard_levels(own_key, shape, split, smallest, top_value):
    factor_of = 1.0
    for axis_at, blocks in split:
        heights = jax.random.uniform(jax.random.fold_in(jax.random.fold_in(own_key, 6), axis_at), (blocks,), jnp.float32, smallest / len(split), top_value / len(split))
        factor_of = factor_of * jnp.repeat(jnp.exp(heights), shape[axis_at] // blocks).reshape((-1,) + (1,) * (len(shape) - 1 - axis_at))
    return factor_of


def rank_table(number_of, skew):
    weights = [(1 << 20) // math.isqrt(rank ** skew) + 1 for rank in range(1, number_of + 1)]
    scale = 1 + sum(weights) // (1 << 30)
    return np.cumsum(np.array([max(1, weight // scale) for weight in weights]))


def skewed_ids(key, shape, count, slope):
    table = rank_table(count, slope)
    pick = jax.random.randint(jax.random.fold_in(key, 1), shape, 0, int(table[count - 1]))
    grade = jnp.searchsorted(jnp.asarray(table, jnp.int32), pick, side="right")
    return jax.random.permutation(jax.random.fold_in(key, 2), count)[grade].astype(jnp.int32)


def gaussian(own_key, dims, scale, most, cuts=(), held_as=jnp.bfloat16):
    level = shard_levels(own_key, dims, cuts, -0.22, 0.18) if cuts else 1.0
    entries = jax.random.normal(own_key, dims, jnp.float32) * scale * level
    return jnp.minimum(jnp.maximum(entries, -most), most).astype(held_as)


def setup_inputs(seed: int = 0) -> dict:
    arg_keys = jax.random.split(jax.random.key(seed), 12)
    return {
        "features": gaussian(arg_keys[0], (C, PARTICLES), 1.0, 6.0, ((1, 128),)),
        "basis_values": gaussian(arg_keys[1], (K, PARTICLES), 1.0, 6.0, ((1, 128),)),
        "positions": jnp.clip(2.0 * jax.random.uniform(arg_keys[2], (3, PARTICLES), jnp.float32) ** shard_levels(arg_keys[2], (3, PARTICLES), ((1, 128),), -0.2, 0.2), 0.0, 2.0),
        "translation": gaussian(arg_keys[3], (LAYERS, NCLASS, K, K), K ** -0.5, 0.75),
        "far_mixing": gaussian(arg_keys[4], (LAYERS, C, C), C ** -0.5, 0.5),
        "near_mixing": gaussian(arg_keys[5], (LAYERS, C, C), C ** -0.5, 0.5),
        "send_box": touch_ends(jax.random.randint(arg_keys[6], (DEVICES, DEVICES, CAP), 0, BOX_DEV), jax.random.fold_in(arg_keys[6], 1), 0, BOX_DEV - 1).astype(jnp.int32),
        "source_dev": touch_ends(skewed_ids(arg_keys[7], (BOXES, L_FAR), DEVICES, 2), jax.random.fold_in(arg_keys[7], 3), 0, DEVICES - 1).astype(jnp.int32),
        "source_slot": touch_ends(jax.random.randint(arg_keys[8], (BOXES, L_FAR), 0, CAP), jax.random.fold_in(arg_keys[8], 1), 0, CAP - 1).astype(jnp.int32),
        "offset_class": touch_ends(jax.random.randint(arg_keys[9], (BOXES, L_FAR), 0, NCLASS), jax.random.fold_in(arg_keys[9], 1), 0, NCLASS - 1).astype(jnp.int32),
        "near_boxes": draw_near_boxes(jax.random.fold_in(arg_keys[11], 71), 0),
    }


softening = 0.25

def kernel_weights(target_pos, source_pos):
    spread = target_pos[:, :, :, None] - source_pos[:, :, None, :]
    square = lax.optimization_barrier(jnp.sum(spread * spread, axis=0))
    return lax.rsqrt(square + softening * softening).astype(jnp.bfloat16)

def reference(features, basis_values, positions, translation, far_mixing, near_mixing, send_box, source_dev, source_slot, offset_class, near_boxes):
    box_block = BOX_DEV
    blocks = BOXES // box_block
    owner_dev = (jnp.arange(BOXES, dtype=jnp.int32) // BOX_DEV)[:, None] + jnp.zeros((1, L_FAR), jnp.int32)
    sources = (source_dev * BOX_DEV + send_box[source_dev, owner_dev, source_slot]).astype(jnp.int32)
    basis_box = basis_values.reshape(K, BOXES, P_SIZE).astype(jnp.float32)
    pos_box = positions.reshape(3, BOXES, P_SIZE)
    target_pos = pos_box.reshape(3, blocks, box_block, P_SIZE).transpose(1, 0, 2, 3)
    source_blocks = sources.reshape(blocks, box_block, L_FAR)
    class_blocks = offset_class.reshape(blocks, box_block, L_FAR)
    near_blocks = near_boxes.reshape(blocks, box_block, L_NEAR)
    current = features
    for section_index in range(LAYERS):
        feat_box = current.reshape(C, BOXES, P_SIZE)
        multipole = (jnp.einsum('kbp,cbp->bkc', basis_box, feat_box.astype(jnp.float32)) * P_SIZE ** (-0.5)).astype(jnp.bfloat16)
        matrices = translation[section_index]

        def far_block(pieces):
            box_ids, class_ids = pieces
            gathered = multipole[box_ids].astype(jnp.float32)
            chosen = matrices[class_ids].astype(jnp.float32)
            return jnp.einsum('bjkm,bjmc->bkc', chosen, gathered) * L_FAR ** (-0.5)
        local_terms = lax.map(far_block, (source_blocks, class_blocks)).reshape(BOXES * K, C)
        mixed_local = jnp.dot(local_terms, far_mixing[section_index].astype(jnp.float32), precision=lax.Precision.HIGHEST).astype(jnp.bfloat16).reshape(BOXES, K, C)
        far_field = (jnp.einsum('bkc,kbp->cbp', mixed_local.astype(jnp.float32), basis_box) * K ** (-0.5)).reshape(C, PARTICLES)

        def near_block(pieces):
            box_ids, here_pos = pieces
            source = feat_box[:, box_ids].reshape(C, box_block, L_NEAR * P_SIZE).astype(jnp.float32)
            source_pos = pos_box[:, box_ids].reshape(3, box_block, L_NEAR * P_SIZE)
            weights = kernel_weights(here_pos, source_pos).astype(jnp.float32)
            return (jnp.einsum('bps,cbs->cbp', weights, source) * (L_NEAR * P_SIZE) ** (-0.5)).astype(jnp.bfloat16)
        near_field = lax.map(near_block, (near_blocks, target_pos)).transpose(1, 0, 2, 3).reshape(C, PARTICLES)
        update = jnp.dot(near_mixing[section_index].T, near_field, preferred_element_type=jnp.float32) + far_field
        current = (current.astype(jnp.float32) + jax.nn.silu(update)).astype(jnp.bfloat16)
    return current
```

```python
import functools

import jax
import jax.numpy as jnp
from jax import lax
from jax.experimental import pallas as pl
from jax.experimental.pallas import tpu as pltpu
from jax.sharding import PartitionSpec as P

LAYERS = 2
L_FAR = 32
L_NEAR = 27
HB = 8
GROUP = 4
WINDOW = GROUP + 2 * HB
ROWS_CNT = 24
ROWS_NEAR = 32
SOFT = 0.25 * 0.25
AXES = ("box", "grp")
BF = jnp.bfloat16
F32 = jnp.float32


def dot(a, b):
    return jnp.dot(a, b, preferred_element_type=F32)


def dot_nt(a, b):
    return lax.dot_general(a, b, (((1,), (1,)), ((), ())), preferred_element_type=F32)


def halo(x, width):
    peers, length = lax.axis_size(AXES), x.shape[1]
    up = [(i, i + 1) for i in range(peers - 1)]
    down = [(j, i) for i, j in up]
    last = lax.slice_in_dim(x, length - width, length, axis=1)
    first = lax.slice_in_dim(x, 0, width, axis=1)
    return jnp.concatenate([lax.ppermute(last, AXES, up), x, lax.ppermute(first, AXES, down)], axis=1)


def block_diagonal(basis):
    k, lanes = basis.shape
    per_box = lanes // GROUP
    rows = lax.broadcasted_iota(jnp.int32, (GROUP * k, lanes), 0) // k
    cols = lax.broadcasted_iota(jnp.int32, (GROUP * k, lanes), 1) // per_box
    stacked = jnp.concatenate([basis] * GROUP, axis=0).astype(F32)
    return jnp.where(rows == cols, stacked, 0.0).astype(BF)


def multipole_of(diag, feat, per_box):
    return (dot_nt(diag, feat) * per_box ** (-0.5)).astype(BF)


def send_all(ids_ref, mult_ref, out_ref, sem):
    def start(i, carry):
        pltpu.make_async_copy(mult_ref.at[ids_ref[i]], out_ref.at[i], sem).start()
        return carry

    lax.fori_loop(0, out_ref.shape[0], start, 0)
    pltpu.make_async_copy(out_ref, out_ref, sem).wait()


def outgoing_kernel(ids_ref, feat_ref, basis_ref, out_ref, mult_ref, sem):
    k = basis_ref.shape[0]
    boxes = mult_ref.shape[0]
    lanes = feat_ref.shape[1] * GROUP // boxes
    for g in range(boxes // GROUP):
        at = pl.ds(g * lanes, lanes)
        diag = block_diagonal(basis_ref[:, at])
        mult = multipole_of(diag, feat_ref[:, at], lanes // GROUP)
        mult_ref[pl.ds(g * GROUP, GROUP)] = mult.reshape(GROUP, k, mult.shape[1])
    send_all(ids_ref, mult_ref, out_ref, sem)


def outgoing_blocks(ids, feat, basis, boxes):
    c = feat.shape[0]
    k = basis.shape[0]
    n = ids.shape[0]
    return pl.pallas_call(
        outgoing_kernel,
        grid_spec=pltpu.PrefetchScalarGridSpec(
            num_scalar_prefetch=1,
            grid=(),
            in_specs=[pl.BlockSpec(memory_space=pltpu.VMEM)] * 2,
            out_specs=pl.BlockSpec(memory_space=pl.ANY),
            scratch_shapes=[pltpu.VMEM((boxes, k, c), BF), pltpu.SemaphoreType.DMA],
        ),
        out_shape=jax.ShapeDtypeStruct((n, k, c), BF),
        compiler_params=pltpu.CompilerParams(vmem_limit_bytes=16 << 20),
        name="outgoing",
    )(ids, feat, basis)


def near_kernel(near_ref, here_ref, there_ref, feat_ref, mix_ref, out_ref, weight_ref, *, per_box, scale):
    g = pl.program_id(0)
    lanes = out_ref.shape[1]
    slot = lax.broadcasted_iota(jnp.int32, (ROWS_CNT, lanes), 0)
    counts = jnp.zeros((ROWS_CNT, lanes), F32)
    for j in range(L_NEAR):
        counts = counts + jnp.where(slot == near_ref[j : j + 1, :], 1.0, 0.0)
    start = pl.multiple_of(g * lanes, lanes)
    px, py, pz = (here_ref[i : i + 1, :] for i in range(3))
    for w in range(WINDOW):
        q = there_ref[pl.ds(start + w * per_box, per_box), :]
        dx = px - q[:, 0:1]
        dy = py - q[:, 1:2]
        dz = pz - q[:, 2:3]
        square = dx * dx + dy * dy + dz * dz
        weight = lax.rsqrt(square + SOFT) * counts[w : w + 1, :]
        weight_ref[pl.ds(w * per_box, per_box), :] = weight.astype(BF)
    source = feat_ref[:, pl.ds(start, WINDOW * per_box)]
    near = (dot(source, weight_ref[...]) * scale).astype(BF)
    out_ref[...] = dot(mix_ref[...], near)


def near_term(near_rel, positions, there, ext_feat, mix_t, boxes):
    particles = positions.shape[1]
    c = ext_feat.shape[0]
    per_box = particles // boxes
    lanes = GROUP * per_box
    whole = pl.BlockSpec(memory_space=pltpu.VMEM)
    elements = particles * WINDOW * per_box
    return pl.pallas_call(
        functools.partial(near_kernel, per_box=per_box, scale=(L_NEAR * per_box) ** (-0.5)),
        grid=(boxes // GROUP,),
        in_specs=[
            pl.BlockSpec((ROWS_NEAR, lanes), lambda g: (0, g)),
            pl.BlockSpec((3, lanes), lambda g: (0, g)),
            whole,
            whole,
            whole,
        ],
        out_specs=pl.BlockSpec((c, lanes), lambda g: (0, g)),
        out_shape=jax.ShapeDtypeStruct((c, particles), F32),
        scratch_shapes=[pltpu.VMEM((WINDOW * per_box, lanes), BF)],
        compiler_params=pltpu.CompilerParams(vmem_limit_bytes=24 << 20),
        cost_estimate=pl.CostEstimate(
            flops=2 * elements * c + 10 * elements,
            bytes_accessed=12 << 20,
            transcendentals=elements,
        ),
        name="near",
    )(near_rel, positions, there, ext_feat, mix_t)


def far_update(g, slot_ref, class_ref, recv_ref, trans_ref, feat_ref, basis_ref, near_ref, mix_ref, out_ref):
    k = basis_ref.shape[0]
    c = feat_ref.shape[0]
    left = lax.broadcasted_iota(jnp.int32, (k, 2 * k), 1) < k
    local = []
    for b in range(GROUP):
        base = (g * GROUP + b) * L_FAR
        total = None
        for quad in range(0, L_FAR, 4):
            ids = [base + quad + i for i in range(4)]
            mats = [trans_ref[class_ref[i]] for i in ids]
            blocks = jnp.concatenate([recv_ref[slot_ref[i]] for i in ids], axis=0)
            lhs = jnp.concatenate(
                [jnp.where(left, mats[0], mats[1]), jnp.where(left, mats[2], mats[3])], axis=1
            )
            part = dot(lhs, blocks)
            total = part if total is None else total + part
        local.append(total * L_FAR ** (-0.5))
    local = jnp.concatenate(local, axis=0)
    high = local.astype(BF)
    low = (local - high.astype(F32)).astype(BF)
    mixed = (dot_nt(mix_ref[...], high) + dot_nt(mix_ref[...], low)).astype(BF)
    diag = block_diagonal(basis_ref[...])
    update = dot(mixed, diag) * k ** (-0.5) + near_ref[...]
    silu = update * (0.5 + 0.5 * jnp.tanh(0.5 * update))
    current = (feat_ref[...].astype(F32) + silu).astype(BF)
    out_ref[...] = current
    return current, diag


def far_last_kernel(slot_ref, class_ref, *refs):
    far_update(pl.program_id(0), slot_ref, class_ref, *refs)


def far_kernel(slot_ref, class_ref, ids_ref, *refs):
    *inner, send_ref, mult_ref, sem = refs
    g = pl.program_id(0)
    current, diag = far_update(g, slot_ref, class_ref, *inner)
    mult = multipole_of(diag, current, current.shape[1] // GROUP)
    mult_ref[pl.ds(g * GROUP, GROUP)] = mult.reshape((GROUP,) + mult_ref.shape[1:])

    @pl.when(g == pl.num_programs(0) - 1)
    def _():
        send_all(ids_ref, mult_ref, send_ref, sem)


def far_term(slots, classes, received, trans, feat, basis, near, mix_t, ids, boxes):
    c, particles = feat.shape
    k = basis.shape[0]
    lanes = GROUP * particles // boxes
    whole = pl.BlockSpec(memory_space=pltpu.VMEM)
    last = ids is None
    scalars = (slots, classes) if last else (slots, classes, ids)
    tile = pl.BlockSpec((c, lanes), lambda g, *_: (0, g))
    out_specs = [tile]
    out_shape = [jax.ShapeDtypeStruct((c, particles), BF)]
    scratch = []
    if not last:
        out_specs.append(pl.BlockSpec(memory_space=pl.ANY))
        out_shape.append(jax.ShapeDtypeStruct((ids.shape[0], k, c), BF))
        scratch = [pltpu.VMEM((boxes, k, c), BF), pltpu.SemaphoreType.DMA]
    return pl.pallas_call(
        far_last_kernel if last else far_kernel,
        grid_spec=pltpu.PrefetchScalarGridSpec(
            num_scalar_prefetch=len(scalars),
            grid=(boxes // GROUP,),
            in_specs=[
                whole,
                whole,
                tile,
                pl.BlockSpec((k, lanes), lambda g, *_: (0, g)),
                tile,
                whole,
            ],
            out_specs=out_specs,
            scratch_shapes=scratch,
        ),
        out_shape=out_shape,
        compiler_params=pltpu.CompilerParams(vmem_limit_bytes=40 << 20),
        name="far_last" if last else "far",
    )(*scalars, received, trans, feat, basis, near, mix_t)


def body(
    features,
    basis_values,
    positions,
    translation,
    far_mixing,
    near_mixing,
    send_box,
    source_dev,
    source_slot,
    offset_class,
    near_boxes,
):
    channels, particles = features.shape
    boxes = source_dev.shape[0]
    per_box = particles // boxes
    capacity = send_box.shape[2]
    device_index = lax.axis_index(AXES)
    ids = send_box.reshape(-1)
    slots = (source_dev * capacity + source_slot).reshape(-1)
    classes = offset_class.reshape(-1)
    trans = jnp.concatenate([translation, translation], axis=-1)
    far_t = far_mixing.transpose(0, 2, 1)
    near_t = near_mixing.transpose(0, 2, 1)
    first_of = (jnp.arange(boxes, dtype=jnp.int32) // GROUP) * GROUP
    near_rel = (near_boxes - device_index * boxes + HB - first_of[:, None]).T
    near_rel = jnp.repeat(near_rel, per_box, axis=1)
    near_rel = jnp.pad(near_rel, ((0, ROWS_NEAR - L_NEAR), (0, 0)), constant_values=-1)
    there = halo(positions, HB * per_box).T
    current = features
    send = outgoing_blocks(ids, features, basis_values, boxes)
    for layer in range(LAYERS):
        received = lax.all_to_all(send, AXES, split_axis=0, concat_axis=0, tiled=True)
        ext_feat = halo(current, HB * per_box)
        near = near_term(near_rel, positions, there, ext_feat, near_t[layer], boxes)
        last = layer == LAYERS - 1
        result = far_term(
            slots,
            classes,
            received,
            trans[layer],
            current,
            basis_values,
            near,
            far_t[layer],
            None if last else ids,
            boxes,
        )
        current = result[0]
        if not last:
            send = result[1]
    return current


def solution(mesh):
    placed = (
        P(None, AXES),
        P(None, AXES),
        P(None, AXES),
        P(),
        P(),
        P(),
        P(AXES, None, None),
        P(AXES, None),
        P(AXES, None),
        P(AXES, None),
        P(AXES, None),
    )
    return jax.shard_map(body, mesh=mesh, in_specs=placed, out_specs=P(None, AXES), check_vma=False)
```

```python
import functools

import jax
import jax.numpy as jnp
from jax import lax
from jax.experimental import pallas as pl
from jax.experimental.pallas import tpu as pltpu
from jax.sharding import PartitionSpec as P

LAYERS = 2
L_FAR = 32
L_NEAR = 27
HB = 8
GROUP = 4
WINDOW = GROUP + 2 * HB
EDGE = HB // GROUP
BATCH = 4
TARGETS = 8
TERMS = 8
ROWS_CNT = 24
ROWS_NEAR = 32
SOFT = 0.25 * 0.25
AXES = ("box", "grp")
BF = jnp.bfloat16
F32 = jnp.float32
VMEM = pl.BlockSpec(memory_space=pltpu.VMEM)
HBM = pl.BlockSpec(memory_space=pltpu.HBM)


def dot(a, b):
    return jnp.dot(a, b, preferred_element_type=F32)


def dot_nt(a, b):
    return lax.dot_general(a, b, (((1,), (1,)), ((), ())), preferred_element_type=F32)


def call(kernel, scalars, args, out_specs, out_shape, scratch, limit, name, cost=None):
    return pl.pallas_call(
        kernel,
        grid_spec=pltpu.PrefetchScalarGridSpec(
            num_scalar_prefetch=len(scalars),
            grid=(),
            in_specs=[VMEM] * len(args),
            out_specs=out_specs,
            scratch_shapes=scratch,
        ),
        out_shape=out_shape,
        compiler_params=pltpu.CompilerParams(vmem_limit_bytes=limit << 20),
        cost_estimate=cost,
        name=name,
    )(*scalars, *args)


def halo(x, width):
    peers, length = lax.axis_size(AXES), x.shape[1]
    up = [(i, i + 1) for i in range(peers - 1)]
    down = [(j, i) for i, j in up]
    last = lax.slice_in_dim(x, length - width, length, axis=1)
    first = lax.slice_in_dim(x, 0, width, axis=1)
    return lax.ppermute(last, AXES, up), lax.ppermute(first, AXES, down)


def block_diagonal(basis):
    k, lanes = basis.shape
    half = lanes // 2
    left = lax.broadcasted_iota(jnp.int32, (k, half), 1) < half // 2
    zero = jnp.zeros((k, half), BF)
    rows = []
    for b in range(GROUP):
        pair = basis[:, (b // 2) * half : (b // 2 + 1) * half]
        own = jnp.where(left, pair, zero) if b % 2 == 0 else jnp.where(left, zero, pair)
        rows.append(jnp.concatenate([own, zero] if b < 2 else [zero, own], axis=1))
    return jnp.concatenate(rows, axis=0)


def store_multipole(mult_ref, g, diag, feat, scale):
    mult = (dot_nt(diag, feat) * scale).astype(BF)
    mult_ref[pl.ds(g * GROUP, GROUP)] = mult.reshape((GROUP,) + mult_ref.shape[1:])


def send_all(ids_ref, mult_ref, out_ref, sem):
    def start(i):
        pltpu.make_async_copy(mult_ref.at[ids_ref[i]], out_ref.at[i], sem).start()

    pl.loop(0, out_ref.shape[0], unroll=8)(start)
    pltpu.make_async_copy(out_ref, out_ref, sem).wait()


def outgoing_kernel(ids_ref, feat_ref, basis_ref, out_ref, mult_ref, sem):
    boxes = mult_ref.shape[0]
    lanes = feat_ref.shape[1] * GROUP // boxes
    scale = (lanes // GROUP) ** (-0.5)

    def step(s):
        for i in range(BATCH):
            g = s * BATCH + i
            at = pl.ds(pl.multiple_of(g * lanes, lanes), lanes)
            store_multipole(mult_ref, g, block_diagonal(basis_ref[:, at]), feat_ref[:, at], scale)

    pl.loop(0, boxes // GROUP // BATCH)(step)
    send_all(ids_ref, mult_ref, out_ref, sem)


def outgoing_blocks(ids, feat, basis, boxes):
    c, k, n = feat.shape[0], basis.shape[0], ids.shape[0]
    return call(
        outgoing_kernel,
        (ids,),
        (feat, basis),
        HBM,
        jax.ShapeDtypeStruct((n, k, c), BF),
        [pltpu.VMEM((boxes, k, c), BF), pltpu.SemaphoreType.DMA],
        16,
        "outgoing",
    )


def counts_of(rel, start):
    slot = lax.broadcasted_iota(jnp.int32, (ROWS_CNT, rel.shape[1]), 0) + start
    counts = jnp.zeros(slot.shape, F32)
    for j in range(L_NEAR):
        counts = counts + jnp.where(slot == rel[j : j + 1, :], 1.0, 0.0)
    return counts


def weights_of(here, there, counts):
    square = None
    for i in range(3):
        d = here[i : i + 1, :] - there[:, i : i + 1]
        square = d * d if square is None else square + d * d
    return (lax.rsqrt(square + SOFT) * counts).astype(BF)


def near_kernel(near_ref, here_ref, there_ref, feat_ref, mix_ref, mid_ref, edge_ref, weight_ref, *, per_box, scale):
    lanes = GROUP * per_box
    groups = feat_ref.shape[1] // lanes

    def own_sum(g):
        first = jnp.clip((g - EDGE) * GROUP, 0, groups * GROUP - WINDOW)
        at = pl.ds(pl.multiple_of(g * lanes, lanes), lanes)
        counts = counts_of(near_ref[:, at], first)
        here = here_ref[:, at]
        start = pl.multiple_of(first * per_box, lanes)
        for w in range(WINDOW):
            there = there_ref[pl.ds(start + w * per_box, per_box), :]
            weight_ref[pl.ds(w * per_box, per_box), :] = weights_of(here, there, counts[w : w + 1, :])
        return dot(feat_ref[:, pl.ds(start, WINDOW * per_box)], weight_ref[...])

    def middle(i):
        near = (own_sum(i + EDGE) * scale).astype(BF)
        mid_ref[:, pl.ds(pl.multiple_of(i * lanes, lanes), lanes)] = dot(mix_ref[...], near)

    def edge(i):
        g = jnp.where(i < EDGE, i, i + groups - 2 * EDGE)
        edge_ref[:, pl.ds(pl.multiple_of(i * lanes, lanes), lanes)] = own_sum(g)

    pl.loop(0, groups - 2 * EDGE)(middle)
    pl.loop(0, 2 * EDGE)(edge)


def near_own(near_rel, positions, there, feat, mix_t, boxes):
    c, particles = feat.shape
    per_box = particles // boxes
    lanes = GROUP * per_box
    elements = particles * WINDOW * per_box
    return call(
        functools.partial(near_kernel, per_box=per_box, scale=(L_NEAR * per_box) ** (-0.5)),
        (),
        (near_rel, positions, there, feat, mix_t),
        [VMEM, VMEM],
        [
            jax.ShapeDtypeStruct((c, particles - 2 * EDGE * lanes), F32),
            jax.ShapeDtypeStruct((c, 2 * EDGE * lanes), F32),
        ],
        [pltpu.VMEM((WINDOW * per_box, lanes), BF)],
        16,
        "near_own",
        pl.CostEstimate(
            flops=2 * elements * c + 10 * elements,
            bytes_accessed=12 << 20,
            transcendentals=elements,
        ),
    )


def edge_weight_kernel(near_ref, here_ref, there_ref, out_ref, *, per_box, boxes):
    lanes = GROUP * per_box
    groups = boxes // GROUP
    for i in range(2 * EDGE):
        low = i < EDGE
        g = i if low else groups - 2 * EDGE + i
        at = pl.ds(g * lanes, lanes)
        counts = counts_of(near_ref[:, at], -HB if low else boxes)
        here = here_ref[:, at]
        for w in range(HB):
            there = there_ref[pl.ds((w if low else HB + w) * per_box, per_box), :]
            out_ref[i, pl.ds(w * per_box, per_box), :] = weights_of(here, there, counts[w : w + 1, :])


def edge_weights(near_rel, positions, there, boxes):
    per_box = positions.shape[1] // boxes
    lanes = GROUP * per_box
    return call(
        functools.partial(edge_weight_kernel, per_box=per_box, boxes=boxes),
        (),
        (near_rel, positions, there),
        VMEM,
        jax.ShapeDtypeStruct((2 * EDGE, HB * per_box, lanes), BF),
        [],
        16,
        "edge_weights",
    )


def near_edge_kernel(weight_ref, before_ref, after_ref, part_ref, mix_ref, out_ref, *, scale):
    lanes = weight_ref.shape[2]
    sums = []
    for i in range(2 * EDGE):
        source = (before_ref if i < EDGE else after_ref)[...]
        sums.append(part_ref[:, i * lanes : (i + 1) * lanes] + dot(source, weight_ref[i]))
    for i, total in enumerate(sums):
        out_ref[:, i * lanes : (i + 1) * lanes] = dot(mix_ref[...], (total * scale).astype(BF))


def near_edge(weights, before, after, part, mix_t, per_box):
    return call(
        functools.partial(near_edge_kernel, scale=(L_NEAR * per_box) ** (-0.5)),
        (),
        (weights, before, after, part, mix_t),
        VMEM,
        jax.ShapeDtypeStruct(part.shape, F32),
        [],
        16,
        "near_edge",
    )


def far_body(slot_ref, class_ref, ids_ref, recv_ref, trans_ref, feat_ref, basis_ref, mid_ref, edge_ref, mix_ref, out_ref, send_ref, local_ref, mult_ref, sem):
    k = basis_ref.shape[0]
    boxes = local_ref.shape[0] // k
    lanes = GROUP * out_ref.shape[1] // boxes
    groups = boxes // GROUP
    left = lax.broadcasted_iota(jnp.int32, (k, 2 * k), 1) < k

    def gather(s):
        for b in range(TARGETS):
            t = s * TARGETS + b
            total = None
            for first in range(0, L_FAR, TERMS):
                ids = [t * L_FAR + first + i for i in range(TERMS)]
                mats = [trans_ref[class_ref[i]] for i in ids]
                pairs = [jnp.where(left, mats[i], mats[i + 1]) for i in range(0, TERMS, 2)]
                blocks = jnp.concatenate([recv_ref[slot_ref[i]] for i in ids], axis=0)
                part = dot(jnp.concatenate(pairs, axis=1), blocks)
                total = part if total is None else total + part
            local_ref[pl.ds(pl.multiple_of(t * k, k), k), :] = total * L_FAR ** (-0.5)

    def tail(which, near):
        at = [pl.ds(pl.multiple_of(g * lanes, lanes), lanes) for g in which]
        rows = [pl.ds(pl.multiple_of(g * GROUP * k, GROUP * k), GROUP * k) for g in which]
        local = [local_ref[r, :] for r in rows]
        high = [x.astype(BF) for x in local]
        low = [(x - h.astype(F32)).astype(BF) for x, h in zip(local, high)]
        mixed = [(dot_nt(mix_ref[...], h) + dot_nt(mix_ref[...], l)).astype(BF) for h, l in zip(high, low)]
        diag = [block_diagonal(basis_ref[:, a]) for a in at]
        update = [dot(m, d) * k ** (-0.5) + n() for m, d, n in zip(mixed, diag, near)]
        current = []
        for u, a in zip(update, at):
            silu = u * (0.5 + 0.5 * jnp.tanh(0.5 * u))
            current.append((feat_ref[:, a].astype(F32) + silu).astype(BF))
            out_ref[:, a] = current[-1]
        if mult_ref is not None:
            for g, d, x in zip(which, diag, current):
                store_multipole(mult_ref, g, d, x, (lanes // GROUP) ** (-0.5))

    def middle(s):
        inner = [s * BATCH + i for i in range(BATCH)]
        near = [
            functools.partial(lambda i: mid_ref[:, pl.ds(pl.multiple_of(i * lanes, lanes), lanes)], i)
            for i in inner
        ]
        tail([i + EDGE for i in inner], near)

    pl.loop(0, boxes // TARGETS)(gather)
    pl.loop(0, (groups - 2 * EDGE) // BATCH)(middle)
    ends = list(range(EDGE)) + list(range(groups - EDGE, groups))
    tail(ends, [functools.partial(lambda i: edge_ref[:, i * lanes : (i + 1) * lanes], i) for i in range(2 * EDGE)])
    if mult_ref is not None:
        send_all(ids_ref, mult_ref, send_ref, sem)


def far_last_kernel(slot_ref, class_ref, *refs):
    *ins, out_ref, local_ref = refs
    far_body(slot_ref, class_ref, None, *ins, out_ref, None, local_ref, None, None)


def far_term(slots, classes, ids, tables, boxes):
    feat, basis = tables[2], tables[3]
    c, particles = feat.shape
    k = basis.shape[0]
    updated = jax.ShapeDtypeStruct((c, particles), BF)
    local = pltpu.VMEM((boxes * k, c), F32)
    if ids is None:
        return call(far_last_kernel, (slots, classes), tables, VMEM, updated, [local], 40, "far_last"), None
    return call(
        far_body,
        (slots, classes, ids),
        tables,
        [VMEM, HBM],
        [updated, jax.ShapeDtypeStruct((ids.shape[0], k, c), BF)],
        [local, pltpu.VMEM((boxes, k, c), BF), pltpu.SemaphoreType.DMA],
        40,
        "far",
    )


def body(
    features,
    basis_values,
    positions,
    translation,
    far_mixing,
    near_mixing,
    send_box,
    source_dev,
    source_slot,
    offset_class,
    near_boxes,
):
    channels, particles = features.shape
    boxes = source_dev.shape[0]
    per_box = particles // boxes
    width = HB * per_box
    capacity = send_box.shape[2]
    ids = send_box.reshape(-1)
    slots = (source_dev * capacity + source_slot).reshape(-1)
    classes = offset_class.reshape(-1)
    trans = jnp.concatenate([translation, translation], axis=-1)
    far_t = far_mixing.transpose(0, 2, 1)
    near_t = near_mixing.transpose(0, 2, 1)
    near_rel = (near_boxes - lax.axis_index(AXES) * boxes).T
    near_rel = jnp.repeat(near_rel, per_box, axis=1)
    near_rel = jnp.pad(near_rel, ((0, ROWS_NEAR - L_NEAR), (0, 0)), constant_values=-(1 << 20))
    current = features
    send = outgoing_blocks(ids, features, basis_values, boxes)
    there = positions.T
    for layer in range(LAYERS):
        received = lax.all_to_all(send, AXES, split_axis=0, concat_axis=0, tiled=True)
        before, after = halo(current, width)
        mid, part = near_own(near_rel, positions, there, current, near_t[layer], boxes)
        if layer == 0:
            ends = jnp.concatenate(halo(positions, width), axis=1).T
            weights = edge_weights(near_rel, positions, ends, boxes)
        edge = near_edge(weights, before, after, part, near_t[layer], per_box)
        tables = (received, trans[layer], current, basis_values, mid, edge, far_t[layer])
        current, send = far_term(slots, classes, None if layer == LAYERS - 1 else ids, tables, boxes)
    return current


def solution(mesh):
    placed = (
        P(None, AXES),
        P(None, AXES),
        P(None, AXES),
        P(),
        P(),
        P(),
        P(AXES, None, None),
        P(AXES, None),
        P(AXES, None),
        P(AXES, None),
        P(AXES, None),
    )
    return jax.shard_map(body, mesh=mesh, in_specs=placed, out_specs=P(None, AXES), check_vma=False)
```

```python
import functools

import jax
import jax.numpy as jnp
from jax import lax
from jax.experimental import pallas as pl
from jax.experimental.pallas import tpu as pltpu
from jax.sharding import PartitionSpec as P

LAYERS = 2
L_FAR = 32
L_NEAR = 27
HB = 8
GROUP = 4
WINDOW = GROUP + 2 * HB
EDGE = HB // GROUP
BATCH = 4
TARGETS = 8
TERMS = 8
ROWS_CNT = 24
ROWS_NEAR = 32
SOFT = 0.25 * 0.25
AXES = ("box", "grp")
BF = jnp.bfloat16
F32 = jnp.float32
VMEM = pl.BlockSpec(memory_space=pltpu.VMEM)


def dot(a, b):
    return jnp.dot(a, b, preferred_element_type=F32)


def dot_nt(a, b):
    return lax.dot_general(a, b, (((1,), (1,)), ((), ())), preferred_element_type=F32)


def call(kernel, scalars, args, out_specs, out_shape, scratch, limit, name, cost=None):
    return pl.pallas_call(
        kernel,
        grid_spec=pltpu.PrefetchScalarGridSpec(
            num_scalar_prefetch=len(scalars),
            grid=(),
            in_specs=[VMEM] * len(args),
            out_specs=out_specs,
            scratch_shapes=scratch,
        ),
        out_shape=out_shape,
        compiler_params=pltpu.CompilerParams(vmem_limit_bytes=limit << 20),
        cost_estimate=cost,
        name=name,
    )(*scalars, *args)


def halo(x, width):
    peers, length = lax.axis_size(AXES), x.shape[1]
    up = [(i, i + 1) for i in range(peers - 1)]
    down = [(j, i) for i, j in up]
    last = lax.slice_in_dim(x, length - width, length, axis=1)
    first = lax.slice_in_dim(x, 0, width, axis=1)
    return lax.ppermute(last, AXES, up), lax.ppermute(first, AXES, down)


def block_diagonal(basis):
    k, lanes = basis.shape
    half = lanes // 2
    left = lax.broadcasted_iota(jnp.int32, (k, half), 1) < half // 2
    zero = jnp.zeros((k, half), BF)
    rows = []
    for b in range(GROUP):
        pair = basis[:, (b // 2) * half : (b // 2 + 1) * half]
        own = jnp.where(left, pair, zero) if b % 2 == 0 else jnp.where(left, zero, pair)
        rows.append(jnp.concatenate([own, zero] if b < 2 else [zero, own], axis=1))
    return jnp.concatenate(rows, axis=0)


def store_multipole(mult_ref, g, diag, feat, scale):
    mult = (dot_nt(diag, feat) * scale).astype(BF)
    mult_ref[pl.ds(g * GROUP, GROUP)] = mult.reshape((GROUP,) + mult_ref.shape[1:])


def send_all(ids_ref, mult_ref, out_ref):
    def copy(i):
        out_ref[i] = mult_ref[ids_ref[i]]

    pl.loop(0, out_ref.shape[0], unroll=8)(copy)


def outgoing_kernel(ids_ref, feat_ref, basis_ref, out_ref, mult_ref):
    boxes = mult_ref.shape[0]
    lanes = feat_ref.shape[1] * GROUP // boxes
    scale = (lanes // GROUP) ** (-0.5)

    def step(s):
        for i in range(BATCH):
            g = s * BATCH + i
            at = pl.ds(pl.multiple_of(g * lanes, lanes), lanes)
            store_multipole(mult_ref, g, block_diagonal(basis_ref[:, at]), feat_ref[:, at], scale)

    pl.loop(0, boxes // GROUP // BATCH)(step)
    send_all(ids_ref, mult_ref, out_ref)


def outgoing_blocks(ids, feat, basis, boxes):
    c, k, n = feat.shape[0], basis.shape[0], ids.shape[0]
    return call(
        outgoing_kernel,
        (ids,),
        (feat, basis),
        VMEM,
        jax.ShapeDtypeStruct((n, k, c), BF),
        [pltpu.VMEM((boxes, k, c), BF)],
        16,
        "outgoing",
    )


def counts_of(rel, start):
    slot = lax.broadcasted_iota(jnp.int32, (ROWS_CNT, rel.shape[1]), 0) + start
    counts = jnp.zeros(slot.shape, F32)
    for j in range(L_NEAR):
        counts = counts + jnp.where(slot == rel[j : j + 1, :], 1.0, 0.0)
    return counts


def weights_of(here, there, counts):
    square = None
    for i in range(3):
        d = here[i : i + 1, :] - there[:, i : i + 1]
        square = d * d if square is None else square + d * d
    return (lax.rsqrt(square + SOFT) * counts).astype(BF)


def near_kernel(near_ref, here_ref, there_ref, feat_ref, mix_ref, mid_ref, edge_ref, weight_ref, *, per_box, scale):
    lanes = GROUP * per_box
    groups = feat_ref.shape[1] // lanes

    def own_sum(g):
        first = jnp.clip((g - EDGE) * GROUP, 0, groups * GROUP - WINDOW)
        at = pl.ds(pl.multiple_of(g * lanes, lanes), lanes)
        counts = counts_of(near_ref[:, at], first)
        here = here_ref[:, at]
        start = pl.multiple_of(first * per_box, lanes)
        for w in range(WINDOW):
            there = there_ref[pl.ds(start + w * per_box, per_box), :]
            weight_ref[pl.ds(w * per_box, per_box), :] = weights_of(here, there, counts[w : w + 1, :])
        return dot(feat_ref[:, pl.ds(start, WINDOW * per_box)], weight_ref[...])

    def middle(i):
        near = (own_sum(i + EDGE) * scale).astype(BF)
        mid_ref[:, pl.ds(pl.multiple_of(i * lanes, lanes), lanes)] = dot(mix_ref[...], near)

    def edge(i):
        g = jnp.where(i < EDGE, i, i + groups - 2 * EDGE)
        edge_ref[:, pl.ds(pl.multiple_of(i * lanes, lanes), lanes)] = own_sum(g)

    pl.loop(0, groups - 2 * EDGE)(middle)
    pl.loop(0, 2 * EDGE)(edge)


def near_own(near_rel, positions, there, feat, mix_t, boxes):
    c, particles = feat.shape
    per_box = particles // boxes
    lanes = GROUP * per_box
    elements = particles * WINDOW * per_box
    return call(
        functools.partial(near_kernel, per_box=per_box, scale=(L_NEAR * per_box) ** (-0.5)),
        (),
        (near_rel, positions, there, feat, mix_t),
        [VMEM, VMEM],
        [
            jax.ShapeDtypeStruct((c, particles - 2 * EDGE * lanes), F32),
            jax.ShapeDtypeStruct((c, 2 * EDGE * lanes), F32),
        ],
        [pltpu.VMEM((WINDOW * per_box, lanes), BF)],
        10,
        "near_own",
        pl.CostEstimate(
            flops=2 * elements * c + 10 * elements,
            bytes_accessed=12 << 20,
            transcendentals=elements,
        ),
    )


def edge_weight_kernel(near_ref, here_ref, there_ref, out_ref, *, per_box, boxes):
    lanes = GROUP * per_box
    groups = boxes // GROUP
    for i in range(2 * EDGE):
        low = i < EDGE
        g = i if low else groups - 2 * EDGE + i
        at = pl.ds(g * lanes, lanes)
        counts = counts_of(near_ref[:, at], -HB if low else boxes)
        here = here_ref[:, at]
        for w in range(HB):
            there = there_ref[pl.ds((w if low else HB + w) * per_box, per_box), :]
            out_ref[i, pl.ds(w * per_box, per_box), :] = weights_of(here, there, counts[w : w + 1, :])


def edge_weights(near_rel, positions, there, boxes):
    per_box = positions.shape[1] // boxes
    lanes = GROUP * per_box
    return call(
        functools.partial(edge_weight_kernel, per_box=per_box, boxes=boxes),
        (),
        (near_rel, positions, there),
        VMEM,
        jax.ShapeDtypeStruct((2 * EDGE, HB * per_box, lanes), BF),
        [],
        8,
        "edge_weights",
    )


def near_edge_kernel(weight_ref, before_ref, after_ref, part_ref, mix_ref, out_ref, *, scale):
    lanes = weight_ref.shape[2]
    sums = []
    for i in range(2 * EDGE):
        source = (before_ref if i < EDGE else after_ref)[...]
        sums.append(part_ref[:, i * lanes : (i + 1) * lanes] + dot(source, weight_ref[i]))
    for i, total in enumerate(sums):
        out_ref[:, i * lanes : (i + 1) * lanes] = dot(mix_ref[...], (total * scale).astype(BF))


def near_edge(weights, before, after, part, mix_t, per_box):
    return call(
        functools.partial(near_edge_kernel, scale=(L_NEAR * per_box) ** (-0.5)),
        (),
        (weights, before, after, part, mix_t),
        VMEM,
        jax.ShapeDtypeStruct(part.shape, F32),
        [],
        8,
        "near_edge",
    )


def far_body(slot_ref, class_ref, ids_ref, recv_ref, trans_ref, feat_ref, basis_ref, mid_ref, edge_ref, mix_ref, out_ref, send_ref, local_ref, mult_ref):
    k = basis_ref.shape[0]
    boxes = local_ref.shape[0] // k
    lanes = GROUP * out_ref.shape[1] // boxes
    groups = boxes // GROUP
    left = lax.broadcasted_iota(jnp.int32, (k, 2 * k), 1) < k

    def gather(s):
        for b in range(TARGETS):
            t = s * TARGETS + b
            total = None
            for first in range(0, L_FAR, TERMS):
                ids = [t * L_FAR + first + i for i in range(TERMS)]
                mats = [trans_ref[class_ref[i]] for i in ids]
                pairs = [jnp.where(left, mats[i], mats[i + 1]) for i in range(0, TERMS, 2)]
                blocks = jnp.concatenate([recv_ref[slot_ref[i]] for i in ids], axis=0)
                part = dot(jnp.concatenate(pairs, axis=1), blocks)
                total = part if total is None else total + part
            local_ref[pl.ds(pl.multiple_of(t * k, k), k), :] = total * L_FAR ** (-0.5)

    def tail(which, near):
        at = [pl.ds(pl.multiple_of(g * lanes, lanes), lanes) for g in which]
        rows = [pl.ds(pl.multiple_of(g * GROUP * k, GROUP * k), GROUP * k) for g in which]
        local = [local_ref[r, :] for r in rows]
        high = [x.astype(BF) for x in local]
        low = [(x - h.astype(F32)).astype(BF) for x, h in zip(local, high)]
        mixed = [(dot_nt(mix_ref[...], h) + dot_nt(mix_ref[...], l)).astype(BF) for h, l in zip(high, low)]
        diag = [block_diagonal(basis_ref[:, a]) for a in at]
        update = [dot(m, d) * k ** (-0.5) + n() for m, d, n in zip(mixed, diag, near)]
        current = []
        for u, a in zip(update, at):
            silu = u * (0.5 + 0.5 * jnp.tanh(0.5 * u))
            current.append((feat_ref[:, a].astype(F32) + silu).astype(BF))
            out_ref[:, a] = current[-1]
        if mult_ref is not None:
            for g, d, x in zip(which, diag, current):
                store_multipole(mult_ref, g, d, x, (lanes // GROUP) ** (-0.5))

    def middle(s):
        inner = [s * BATCH + i for i in range(BATCH)]
        near = [
            functools.partial(lambda i: mid_ref[:, pl.ds(pl.multiple_of(i * lanes, lanes), lanes)], i)
            for i in inner
        ]
        tail([i + EDGE for i in inner], near)

    pl.loop(0, boxes // TARGETS)(gather)
    pl.loop(0, (groups - 2 * EDGE) // BATCH)(middle)
    ends = list(range(EDGE)) + list(range(groups - EDGE, groups))
    tail(ends, [functools.partial(lambda i: edge_ref[:, i * lanes : (i + 1) * lanes], i) for i in range(2 * EDGE)])
    if mult_ref is not None:
        send_all(ids_ref, mult_ref, send_ref)


def far_last_kernel(slot_ref, class_ref, *refs):
    *ins, out_ref, local_ref = refs
    far_body(slot_ref, class_ref, None, *ins, out_ref, None, local_ref, None)


def far_term(slots, classes, ids, tables, boxes):
    feat, basis = tables[2], tables[3]
    c, particles = feat.shape
    k = basis.shape[0]
    updated = jax.ShapeDtypeStruct((c, particles), BF)
    local = pltpu.VMEM((boxes * k, c), F32)
    if ids is None:
        return call(far_last_kernel, (slots, classes), tables, VMEM, updated, [local], 24, "far_last"), None
    return call(
        far_body,
        (slots, classes, ids),
        tables,
        [VMEM, VMEM],
        [updated, jax.ShapeDtypeStruct((ids.shape[0], k, c), BF)],
        [local, pltpu.VMEM((boxes, k, c), BF)],
        32,
        "far",
    )


def body(
    features,
    basis_values,
    positions,
    translation,
    far_mixing,
    near_mixing,
    send_box,
    source_dev,
    source_slot,
    offset_class,
    near_boxes,
):
    channels, particles = features.shape
    boxes = source_dev.shape[0]
    per_box = particles // boxes
    width = HB * per_box
    capacity = send_box.shape[2]
    ids = send_box.reshape(-1)
    slots = (source_dev * capacity + source_slot).reshape(-1)
    classes = offset_class.reshape(-1)
    trans = jnp.concatenate([translation, translation], axis=-1)
    far_t = far_mixing.transpose(0, 2, 1)
    near_t = near_mixing.transpose(0, 2, 1)
    near_rel = (near_boxes - lax.axis_index(AXES) * boxes).T
    near_rel = jnp.repeat(near_rel, per_box, axis=1)
    near_rel = jnp.pad(near_rel, ((0, ROWS_NEAR - L_NEAR), (0, 0)), constant_values=-(1 << 20))
    current = features
    send = outgoing_blocks(ids, features, basis_values, boxes)
    there = positions.T
    for layer in range(LAYERS):
        received = lax.all_to_all(send, AXES, split_axis=0, concat_axis=0, tiled=True)
        before, after = halo(current, width)
        mid, part = near_own(near_rel, positions, there, current, near_t[layer], boxes)
        if layer == 0:
            ends = jnp.concatenate(halo(positions, width), axis=1).T
            weights = edge_weights(near_rel, positions, ends, boxes)
        edge = near_edge(weights, before, after, part, near_t[layer], per_box)
        tables = (received, trans[layer], current, basis_values, mid, edge, far_t[layer])
        current, send = far_term(slots, classes, None if layer == LAYERS - 1 else ids, tables, boxes)
    return current


def solution(mesh):
    placed = (
        P(None, AXES),
        P(None, AXES),
        P(None, AXES),
        P(),
        P(),
        P(),
        P(AXES, None, None),
        P(AXES, None),
        P(AXES, None),
        P(AXES, None),
        P(AXES, None),
    )
    return jax.shard_map(body, mesh=mesh, in_specs=placed, out_specs=P(None, AXES), check_vma=False)
```

```python
import functools

import jax
import jax.numpy as jnp
from jax import lax
from jax.experimental import pallas as pl
from jax.experimental.pallas import tpu as pltpu
from jax.sharding import PartitionSpec as P

LAYERS = 2
L_FAR = 32
L_NEAR = 27
HB = 8
GROUP = 4
WINDOW = GROUP + 2 * HB
EDGE = HB // GROUP
BATCH = 4
TARGETS = 16
TERMS = 8
ROWS_CNT = 24
ROWS_NEAR = 32
SOFT = 0.25 * 0.25
AXES = ("box", "grp")
BF = jnp.bfloat16
F32 = jnp.float32
VMEM = pl.BlockSpec(memory_space=pltpu.VMEM)
ANY = pl.BlockSpec(memory_space=pl.ANY)
UNPACK = 79
SENDS = 8
ALL_VMEM = 60


def dot(a, b):
    return jnp.dot(a, b, preferred_element_type=F32)


def dot_nt(a, b):
    return lax.dot_general(a, b, (((1,), (1,)), ((), ())), preferred_element_type=F32)


def call(kernel, args, out_specs, out_shape, scratch, name, limit=None, cost=None):
    return pl.pallas_call(
        kernel,
        grid_spec=pltpu.PrefetchScalarGridSpec(
            num_scalar_prefetch=0,
            grid=(),
            in_specs=[ANY if limit is None else VMEM] * len(args),
            out_specs=out_specs,
            scratch_shapes=scratch,
        ),
        out_shape=out_shape,
        compiler_params=pltpu.CompilerParams(vmem_limit_bytes=(ALL_VMEM if limit is None else limit) << 20),
        cost_estimate=cost,
        name=name,
    )(*args)


def halo(x, width):
    peers, length = lax.axis_size(AXES), x.shape[1]
    up = [(i, i + 1) for i in range(peers - 1)]
    down = [(j, i) for i, j in up]
    last = lax.slice_in_dim(x, length - width, length, axis=1)
    first = lax.slice_in_dim(x, 0, width, axis=1)
    return lax.ppermute(last, AXES, up), lax.ppermute(first, AXES, down)


def block_diagonal(basis):
    k, lanes = basis.shape
    half = lanes // 2
    left = lax.broadcasted_iota(jnp.int32, (k, half), 1) < half // 2
    zero = jnp.zeros((k, half), BF)
    rows = []
    for b in range(GROUP):
        pair = basis[:, (b // 2) * half : (b // 2 + 1) * half]
        own = jnp.where(left, pair, zero) if b % 2 == 0 else jnp.where(left, zero, pair)
        rows.append(jnp.concatenate([own, zero] if b < 2 else [zero, own], axis=1))
    return jnp.concatenate(rows, axis=0)


def store_multipole(mult_ref, g, diag, feat, scale):
    mult = (dot_nt(diag, feat) * scale).astype(BF)
    mult_ref[pl.ds(g * GROUP, GROUP)] = mult.reshape((GROUP,) + mult_ref.shape[1:])


def send_all(ids_ref, mult_ref, stage_ref, out_ref, sem):
    n = out_ref.shape[0]
    capacity = ids_ref.shape[0]
    chunk = n // SENDS
    copies = []
    for s in range(SENDS):

        def put(i):
            for slot in range(capacity):
                target = s * chunk // capacity + i
                stage_ref[target * capacity + slot] = mult_ref[ids_ref[slot, target]]

        pl.loop(0, chunk // capacity, unroll=4)(put)
        at = pl.ds(s * chunk, chunk)
        copies.append(pltpu.make_async_copy(stage_ref.at[at], out_ref.at[at], sem.at[s]))
        copies[-1].start()
    for copy in copies:
        copy.wait()


def outgoing_kernel(ids_hbm, feat_hbm, basis_hbm, out_ref, ids_ref, feat_ref, basis_ref, mult_ref, stage_ref, in_sem, sem):
    boxes = mult_ref.shape[0]
    lanes = feat_ref.shape[1] * GROUP // boxes
    scale = (lanes // GROUP) ** (-0.5)
    steps = boxes // GROUP // BATCH
    copies = []
    for s in range(steps):
        at = pl.ds(s * BATCH * lanes, BATCH * lanes)
        pair = [
            pltpu.make_async_copy(hbm.at[:, at], ref.at[:, at], in_sem.at[2 * s + i])
            for i, (hbm, ref) in enumerate(((basis_hbm, basis_ref), (feat_hbm, feat_ref)))
        ]
        for copy in pair:
            copy.start()
        copies.append(pair)
    ids_copy = pltpu.make_async_copy(ids_hbm, ids_ref, in_sem.at[2 * steps])
    ids_copy.start()
    for s in range(steps):
        for copy in copies[s]:
            copy.wait()
        for i in range(BATCH):
            g = s * BATCH + i
            at = pl.ds(g * lanes, lanes)
            store_multipole(mult_ref, g, block_diagonal(basis_ref[:, at]), feat_ref[:, at], scale)
    ids_copy.wait()
    send_all(ids_ref, mult_ref, stage_ref, out_ref, sem)


def outgoing_blocks(ids, feat, basis, boxes):
    c, k, n = feat.shape[0], basis.shape[0], ids.size
    return call(
        outgoing_kernel,
        (ids, feat, basis),
        ANY,
        jax.ShapeDtypeStruct((n, k, c), BF),
        [
            pltpu.SMEM(ids.shape, jnp.int32),
            pltpu.VMEM(feat.shape, BF),
            pltpu.VMEM(basis.shape, BF),
            pltpu.VMEM((boxes, k, c), BF),
            pltpu.VMEM((n, k, c), BF),
            pltpu.SemaphoreType.DMA((2 * (boxes // GROUP // BATCH) + 1,)),
            pltpu.SemaphoreType.DMA((SENDS,)),
        ],
        "outgoing",
    )


def counts_of(rel, start):
    slot = lax.broadcasted_iota(jnp.int32, (ROWS_CNT, rel.shape[1]), 0) + start
    counts = jnp.zeros(slot.shape, F32)
    for j in range(L_NEAR):
        counts = counts + jnp.where(slot == rel[j : j + 1, :], 1.0, 0.0)
    return counts


def weights_of(here, there, counts):
    square = None
    for i in range(3):
        d = here[i : i + 1, :] - there[:, i : i + 1]
        square = d * d if square is None else square + d * d
    return (lax.rsqrt(square + SOFT) * counts).astype(BF)


def near_kernel(near_ref, here_ref, there_ref, feat_ref, mix_ref, mid_ref, edge_ref, weight_ref, *, per_box, scale):
    lanes = GROUP * per_box
    groups = feat_ref.shape[1] // lanes

    def own_sum(g):
        first = jnp.clip((g - EDGE) * GROUP, 0, groups * GROUP - WINDOW)
        at = pl.ds(pl.multiple_of(g * lanes, lanes), lanes)
        counts = counts_of(near_ref[:, at], first)
        here = here_ref[:, at]
        start = pl.multiple_of(first * per_box, lanes)
        for w in range(WINDOW):
            there = there_ref[pl.ds(start + w * per_box, per_box), :]
            weight_ref[pl.ds(w * per_box, per_box), :] = weights_of(here, there, counts[w : w + 1, :])
        return dot(feat_ref[:, pl.ds(start, WINDOW * per_box)], weight_ref[...])

    def middle(i):
        near = (own_sum(i + EDGE) * scale).astype(BF)
        mid_ref[:, pl.ds(pl.multiple_of(i * lanes, lanes), lanes)] = dot(mix_ref[...], near)

    def edge(i):
        g = jnp.where(i < EDGE, i, i + groups - 2 * EDGE)
        edge_ref[:, pl.ds(pl.multiple_of(i * lanes, lanes), lanes)] = own_sum(g)

    pl.loop(0, groups - 2 * EDGE)(middle)
    pl.loop(0, 2 * EDGE)(edge)


def near_own(near_rel, positions, there, feat, mix_t, boxes):
    c, particles = feat.shape
    per_box = particles // boxes
    lanes = GROUP * per_box
    elements = particles * WINDOW * per_box
    return call(
        functools.partial(near_kernel, per_box=per_box, scale=(L_NEAR * per_box) ** (-0.5)),
        (near_rel, positions, there, feat, mix_t),
        [VMEM, VMEM],
        [
            jax.ShapeDtypeStruct((c, particles - 2 * EDGE * lanes), F32),
            jax.ShapeDtypeStruct((c, 2 * EDGE * lanes), F32),
        ],
        [pltpu.VMEM((WINDOW * per_box, lanes), BF)],
        "near_own",
        10,
        pl.CostEstimate(
            flops=2 * elements * c + 10 * elements,
            bytes_accessed=12 << 20,
            transcendentals=elements,
        ),
    )


def edge_weight_kernel(near_ref, here_ref, there_ref, out_ref, *, per_box, boxes):
    lanes = GROUP * per_box
    groups = boxes // GROUP
    for i in range(2 * EDGE):
        low = i < EDGE
        g = i if low else groups - 2 * EDGE + i
        at = pl.ds(g * lanes, lanes)
        counts = counts_of(near_ref[:, at], -HB if low else boxes)
        here = here_ref[:, at]
        for w in range(HB):
            there = there_ref[pl.ds((w if low else HB + w) * per_box, per_box), :]
            out_ref[i, pl.ds(w * per_box, per_box), :] = weights_of(here, there, counts[w : w + 1, :])


def edge_weights(near_rel, positions, there, boxes):
    per_box = positions.shape[1] // boxes
    lanes = GROUP * per_box
    return call(
        functools.partial(edge_weight_kernel, per_box=per_box, boxes=boxes),
        (near_rel, positions, there),
        VMEM,
        jax.ShapeDtypeStruct((2 * EDGE, HB * per_box, lanes), BF),
        [],
        "edge_weights",
        8,
    )


def near_edge_kernel(weight_ref, before_ref, after_ref, part_ref, mix_ref, out_ref, *, scale):
    lanes = weight_ref.shape[2]
    sums = []
    for i in range(2 * EDGE):
        source = (before_ref if i < EDGE else after_ref)[...]
        sums.append(part_ref[:, i * lanes : (i + 1) * lanes] + dot(source, weight_ref[i]))
    for i, total in enumerate(sums):
        out_ref[:, i * lanes : (i + 1) * lanes] = dot(mix_ref[...], (total * scale).astype(BF))


def near_edge(weights, before, after, part, mix_t, per_box):
    return call(
        functools.partial(near_edge_kernel, scale=(L_NEAR * per_box) ** (-0.5)),
        (weights, before, after, part, mix_t),
        VMEM,
        jax.ShapeDtypeStruct(part.shape, F32),
        [],
        "near_edge",
        8,
    )


def far_body(
    slot_hbm,
    class_hbm,
    ids_hbm,
    recv_hbm,
    trans_hbm,
    feat_hbm,
    basis_hbm,
    mid_hbm,
    edge_hbm,
    mix_hbm,
    out_hbm,
    send_ref,
    slot_ref,
    class_ref,
    pack_ref,
    recv_ref,
    trans_ref,
    feat_ref,
    basis_ref,
    mid_ref,
    edge_ref,
    mix_ref,
    out_ref,
    local_ref,
    in_sem,
    out_sem,
    ids_ref=None,
    mult_ref=None,
    stage_ref=None,
    send_sem=None,
    *,
    layer,
):
    k = basis_ref.shape[0]
    boxes = local_ref.shape[0] // k
    lanes = GROUP * out_ref.shape[1] // boxes
    groups = boxes // GROUP
    left = lax.broadcasted_iota(jnp.int32, (k, 2 * k), 1) < k
    sources = (slot_hbm, class_hbm, trans_hbm.at[layer], recv_hbm, basis_hbm, mid_hbm, feat_hbm, edge_hbm, mix_hbm.at[layer])
    targets = (slot_ref, class_ref, pack_ref, recv_ref, basis_ref, mid_ref, feat_ref, edge_ref, mix_ref)
    if ids_ref is not None:
        sources, targets = sources + (ids_hbm,), targets + (ids_ref,)
    copies = [pltpu.make_async_copy(x, y, in_sem.at[i]) for i, (x, y) in enumerate(zip(sources, targets))]
    for copy in copies:
        copy.start()

    def unpack(i):
        for j in range(UNPACK):
            pack = pack_ref[i * UNPACK + j]
            swap = jnp.concatenate([pack[:, k:], pack[:, :k]], axis=1)
            half = left[: k // 2]
            trans_ref[i * UNPACK + j] = jnp.concatenate(
                [jnp.where(half, pack, swap), jnp.where(half, swap, pack)], axis=0
            )

    def gather(s):
        for b in range(TARGETS):
            t = s * TARGETS + b
            total = None
            for first in range(0, L_FAR, TERMS):
                ids = [t * L_FAR + first + i for i in range(TERMS)]
                mats = [trans_ref[class_ref[i]] for i in ids]
                pairs = [jnp.where(left, mats[i], mats[i + 1]) for i in range(0, TERMS, 2)]
                blocks = jnp.concatenate([recv_ref[slot_ref[i]] for i in ids], axis=0)
                part = dot(jnp.concatenate(pairs, axis=1), blocks)
                total = part if total is None else total + part
            local_ref[pl.ds(pl.multiple_of(t * k, k), k), :] = (total * L_FAR ** (-0.5)).astype(BF)

    def tail(which, near):
        at = [pl.ds(pl.multiple_of(g * lanes, lanes), lanes) for g in which]
        rows = [pl.ds(pl.multiple_of(g * GROUP * k, GROUP * k), GROUP * k) for g in which]
        local = [local_ref[r, :] for r in rows]
        mixed = [dot_nt(mix_ref[...], x).astype(BF) for x in local]
        diag = [block_diagonal(basis_ref[:, a]) for a in at]
        update = [dot(m, d) * k ** (-0.5) + n[...] for m, d, n in zip(mixed, diag, near)]
        current = []
        for u, a in zip(update, at):
            silu = u * (0.5 + 0.5 * jnp.tanh(0.5 * u))
            current.append((feat_ref[:, a].astype(F32) + silu).astype(BF))
            out_ref[:, a] = current[-1]
        if mult_ref is not None:
            for g, d, x in zip(which, diag, current):
                store_multipole(mult_ref, g, d, x, (lanes // GROUP) ** (-0.5))

    copies[2].wait()
    pl.loop(0, pack_ref.shape[0] // UNPACK)(unpack)
    for i in (0, 1, 3):
        copies[i].wait()
    pl.loop(0, boxes // TARGETS)(gather)
    for copy in copies[4:]:
        copy.wait()
    stores = [
        pltpu.make_async_copy(
            out_ref.at[:, pl.ds(first * lanes, count * lanes)],
            out_hbm.at[:, pl.ds(first * lanes, count * lanes)],
            out_sem.at[i],
        )
        for i, (first, count) in enumerate(((EDGE, groups - 2 * EDGE), (0, EDGE), (groups - EDGE, EDGE)))
    ]

    def middle(s):
        inner = [s * BATCH + i for i in range(BATCH)]
        tail(
            [i + EDGE for i in inner],
            [mid_ref.at[:, pl.ds(pl.multiple_of(i * lanes, lanes), lanes)] for i in inner],
        )

    pl.loop(0, (groups - 2 * EDGE) // BATCH)(middle)
    stores[0].start()
    ends = list(range(EDGE)) + list(range(groups - EDGE, groups))
    tail(ends, [edge_ref.at[:, pl.ds(i * lanes, lanes)] for i in range(2 * EDGE)])
    for copy in stores[1:]:
        copy.start()
    if mult_ref is not None:
        send_all(ids_ref, mult_ref, stage_ref, send_ref, send_sem)
    for copy in stores:
        copy.wait()


def far_last_kernel(slot_hbm, class_hbm, *refs, layer):
    ins, out_ref, scratch = refs[:7], refs[7], refs[8:]
    far_body(slot_hbm, class_hbm, None, *ins, out_ref, None, *scratch, layer=layer)


def far_term(slots, classes, ids, tables, boxes, layer):
    recv, pack, feat, basis, mid, edge, mix = tables
    c, particles = feat.shape
    k = basis.shape[0]
    updated = jax.ShapeDtypeStruct((c, particles), BF)
    scratch = [
        pltpu.SMEM(slots.shape, jnp.int32),
        pltpu.SMEM(classes.shape, jnp.int32),
        pltpu.VMEM(pack.shape[1:], BF),
        pltpu.VMEM(recv.shape, BF),
        pltpu.VMEM((pack.shape[1], k, 2 * k), BF),
        pltpu.VMEM(feat.shape, BF),
        pltpu.VMEM(basis.shape, BF),
        pltpu.VMEM(mid.shape, F32),
        pltpu.VMEM(edge.shape, F32),
        pltpu.VMEM(mix.shape[1:], BF),
        pltpu.VMEM(feat.shape, BF),
        pltpu.VMEM((boxes * k, c), BF),
        pltpu.SemaphoreType.DMA((10,)),
        pltpu.SemaphoreType.DMA((3,)),
    ]
    if ids is None:
        kernel = functools.partial(far_last_kernel, layer=layer)
        return call(kernel, (slots, classes) + tables, ANY, updated, scratch, "far_last"), None
    n = ids.size
    scratch += [
        pltpu.SMEM(ids.shape, jnp.int32),
        pltpu.VMEM((boxes, k, c), BF),
        pltpu.VMEM((n, k, c), BF),
        pltpu.SemaphoreType.DMA((SENDS,)),
    ]
    return call(
        functools.partial(far_body, layer=layer),
        (slots, classes, ids) + tables,
        [ANY, ANY],
        [updated, jax.ShapeDtypeStruct((n, k, c), BF)],
        scratch,
        "far",
    )


def body(
    features,
    basis_values,
    positions,
    translation,
    far_mixing,
    near_mixing,
    send_box,
    source_dev,
    source_slot,
    offset_class,
    near_boxes,
):
    channels, particles = features.shape
    boxes = source_dev.shape[0]
    per_box = particles // boxes
    width = HB * per_box
    capacity = send_box.shape[2]
    ids = send_box[0].T
    slots = (source_dev * capacity + source_slot).reshape(-1)
    classes = offset_class.reshape(-1)
    half = translation.shape[2] // 2
    trans = jnp.concatenate([translation[:, :, :half], translation[:, :, half:]], axis=-1)
    far_t = far_mixing.transpose(0, 2, 1)
    near_t = near_mixing.transpose(0, 2, 1)
    near_rel = (near_boxes - lax.axis_index(AXES) * boxes).T
    near_rel = jnp.repeat(near_rel, per_box, axis=1)
    near_rel = jnp.pad(near_rel, ((0, ROWS_NEAR - L_NEAR), (0, 0)), constant_values=-(1 << 20))
    current = features
    send = outgoing_blocks(ids, features, basis_values, boxes)
    there = positions.T
    for layer in range(LAYERS):
        received = lax.all_to_all(send, AXES, split_axis=0, concat_axis=0, tiled=True)
        before, after = halo(current, width)
        mid, part = near_own(near_rel, positions, there, current, near_t[layer], boxes)
        if layer == 0:
            ends = jnp.concatenate(halo(positions, width), axis=1).T
            weights = edge_weights(near_rel, positions, ends, boxes)
        edge = near_edge(weights, before, after, part, near_t[layer], per_box)
        tables = (received, trans, current, basis_values, mid, edge, far_t)
        current, send = far_term(slots, classes, None if layer == LAYERS - 1 else ids, tables, boxes, layer)
    return current


def solution(mesh):
    placed = (
        P(None, AXES),
        P(None, AXES),
        P(None, AXES),
        P(),
        P(),
        P(),
        P(AXES, None, None),
        P(AXES, None),
        P(AXES, None),
        P(AXES, None),
        P(AXES, None),
    )
    return jax.shard_map(body, mesh=mesh, in_specs=placed, out_specs=P(None, AXES), check_vma=False)
```

```python
import functools

import jax
import jax.numpy as jnp
from jax import lax
from jax.experimental import pallas as pl
from jax.experimental.pallas import tpu as pltpu
from jax.sharding import PartitionSpec as P

LAYERS = 2
L_FAR = 32
L_NEAR = 27
HB = 8
GROUP = 4
WINDOW = GROUP + 2 * HB
EDGE = HB // GROUP
BATCH = 4
TARGETS = 16
TERMS = 8
ROWS_CNT = 24
ROWS_NEAR = 32
SOFT = 0.25 * 0.25
AXES = ("box", "grp")
BF = jnp.bfloat16
F32 = jnp.float32
VMEM = pl.BlockSpec(memory_space=pltpu.VMEM)
ANY = pl.BlockSpec(memory_space=pl.ANY)
UNPACK = 79
SIDE = 4
SENDS = 8
ALL_VMEM = 60


def dot(a, b):
    return jnp.dot(a, b, preferred_element_type=F32)


def dot_nt(a, b):
    return lax.dot_general(a, b, (((1,), (1,)), ((), ())), preferred_element_type=F32)


def call(kernel, args, out_specs, out_shape, scratch, name, limit=None, cost=None):
    return pl.pallas_call(
        kernel,
        grid_spec=pltpu.PrefetchScalarGridSpec(
            num_scalar_prefetch=0,
            grid=(),
            in_specs=[ANY if limit is None else VMEM] * len(args),
            out_specs=out_specs,
            scratch_shapes=scratch,
        ),
        out_shape=out_shape,
        compiler_params=pltpu.CompilerParams(vmem_limit_bytes=(ALL_VMEM if limit is None else limit) << 20),
        cost_estimate=cost,
        name=name,
    )(*args)


def halo(x, width):
    peers, length = lax.axis_size(AXES), x.shape[1]
    up = [(i, i + 1) for i in range(peers - 1)]
    down = [(j, i) for i, j in up]
    last = lax.slice_in_dim(x, length - width, length, axis=1)
    first = lax.slice_in_dim(x, 0, width, axis=1)
    return lax.ppermute(last, AXES, up), lax.ppermute(first, AXES, down)


def block_diagonal(basis):
    k, lanes = basis.shape
    half = lanes // 2
    left = lax.broadcasted_iota(jnp.int32, (k, half), 1) < half // 2
    zero = jnp.zeros((k, half), BF)
    rows = []
    for b in range(GROUP):
        pair = basis[:, (b // 2) * half : (b // 2 + 1) * half]
        own = jnp.where(left, pair, zero) if b % 2 == 0 else jnp.where(left, zero, pair)
        rows.append(jnp.concatenate([own, zero] if b < 2 else [zero, own], axis=1))
    return jnp.concatenate(rows, axis=0)


def store_multipole(mult_ref, g, diag, feat, scale):
    mult = (dot_nt(diag, feat) * scale).astype(BF)
    mult_ref[pl.ds(g * GROUP, GROUP)] = mult.reshape((GROUP,) + mult_ref.shape[1:])


def device_at(c, core, b, a):
    x, y, z = a, (a + b) % SIDE, (a + b + c) % SIDE
    return ((z * SIDE + y) * 2 + core) * SIDE + x


def place_of(device):
    x, box = device % SIDE, device // SIDE
    core, y, z = box % 2, box // 2 % SIDE, box // (2 * SIDE)
    return ((((z - y) % SIDE) * 2 + core) * SIDE + (y - x) % SIDE) * SIDE + x


def exchange(blocks):
    order = [device_at(c, core, b, a) for c in range(SIDE) for core in range(2) for b in range(SIDE) for a in range(SIDE)]
    return lax.all_to_all(blocks, AXES, split_axis=0, concat_axis=0, axis_index_groups=[order], tiled=True)


def send_all(ids_ref, mult_ref, stage_ref, out_ref, sem):
    n = out_ref.shape[0]
    capacity = ids_ref.shape[0]
    chunk = n // SENDS
    copies = []
    for s in range(SENDS):

        def put(i):
            for j in range(SIDE):
                place = s * (chunk // capacity) + i * SIDE + j
                target = device_at(s // 2, s % 2, i, j)
                for slot in range(capacity):
                    stage_ref[place * capacity + slot] = mult_ref[ids_ref[slot, target]]

        pl.loop(0, chunk // capacity // SIDE, unroll=2)(put)
        at = pl.ds(s * chunk, chunk)
        copies.append(pltpu.make_async_copy(stage_ref.at[at], out_ref.at[at], sem.at[s]))
        copies[-1].start()
    for copy in copies:
        copy.wait()


def outgoing_kernel(ids_hbm, feat_hbm, basis_hbm, out_ref, ids_ref, feat_ref, basis_ref, mult_ref, stage_ref, in_sem, sem):
    boxes = mult_ref.shape[0]
    lanes = feat_ref.shape[1] * GROUP // boxes
    scale = (lanes // GROUP) ** (-0.5)
    steps = boxes // GROUP // BATCH
    copies = []
    for s in range(steps):
        at = pl.ds(s * BATCH * lanes, BATCH * lanes)
        pair = [
            pltpu.make_async_copy(hbm.at[:, at], ref.at[:, at], in_sem.at[2 * s + i])
            for i, (hbm, ref) in enumerate(((basis_hbm, basis_ref), (feat_hbm, feat_ref)))
        ]
        for copy in pair:
            copy.start()
        copies.append(pair)
    ids_copy = pltpu.make_async_copy(ids_hbm, ids_ref, in_sem.at[2 * steps])
    ids_copy.start()
    for s in range(steps):
        for copy in copies[s]:
            copy.wait()
        for i in range(BATCH):
            g = s * BATCH + i
            at = pl.ds(g * lanes, lanes)
            store_multipole(mult_ref, g, block_diagonal(basis_ref[:, at]), feat_ref[:, at], scale)
    ids_copy.wait()
    send_all(ids_ref, mult_ref, stage_ref, out_ref, sem)


def outgoing_blocks(ids, feat, basis, boxes):
    c, k, n = feat.shape[0], basis.shape[0], ids.size
    return call(
        outgoing_kernel,
        (ids, feat, basis),
        ANY,
        jax.ShapeDtypeStruct((n, k, c), BF),
        [
            pltpu.SMEM(ids.shape, jnp.int32),
            pltpu.VMEM(feat.shape, BF),
            pltpu.VMEM(basis.shape, BF),
            pltpu.VMEM((boxes, k, c), BF),
            pltpu.VMEM((n, k, c), BF),
            pltpu.SemaphoreType.DMA((2 * (boxes // GROUP // BATCH) + 1,)),
            pltpu.SemaphoreType.DMA((SENDS,)),
        ],
        "outgoing",
    )


def counts_of(rel, start):
    slot = lax.broadcasted_iota(jnp.int32, (ROWS_CNT, rel.shape[1]), 0) + start
    counts = jnp.zeros(slot.shape, F32)
    for j in range(L_NEAR):
        counts = counts + jnp.where(slot == rel[j : j + 1, :], 1.0, 0.0)
    return counts


def weights_of(here, there, counts):
    square = None
    for i in range(3):
        d = here[i : i + 1, :] - there[:, i : i + 1]
        square = d * d if square is None else square + d * d
    return (lax.rsqrt(square + SOFT) * counts).astype(BF)


def near_kernel(near_ref, here_ref, there_ref, feat_ref, mix_ref, mid_ref, edge_ref, weight_ref, *, per_box, scale):
    lanes = GROUP * per_box
    groups = feat_ref.shape[1] // lanes

    def own_sum(g):
        first = jnp.clip((g - EDGE) * GROUP, 0, groups * GROUP - WINDOW)
        at = pl.ds(pl.multiple_of(g * lanes, lanes), lanes)
        counts = counts_of(near_ref[:, at], first)
        here = here_ref[:, at]
        start = pl.multiple_of(first * per_box, lanes)
        for w in range(WINDOW):
            there = there_ref[pl.ds(start + w * per_box, per_box), :]
            weight_ref[pl.ds(w * per_box, per_box), :] = weights_of(here, there, counts[w : w + 1, :])
        return dot(feat_ref[:, pl.ds(start, WINDOW * per_box)], weight_ref[...])

    def middle(i):
        near = (own_sum(i + EDGE) * scale).astype(BF)
        mid_ref[:, pl.ds(pl.multiple_of(i * lanes, lanes), lanes)] = dot(mix_ref[...], near)

    def edge(i):
        g = jnp.where(i < EDGE, i, i + groups - 2 * EDGE)
        edge_ref[:, pl.ds(pl.multiple_of(i * lanes, lanes), lanes)] = own_sum(g)

    pl.loop(0, groups - 2 * EDGE)(middle)
    pl.loop(0, 2 * EDGE)(edge)


def near_own(near_rel, positions, there, feat, mix_t, boxes):
    c, particles = feat.shape
    per_box = particles // boxes
    lanes = GROUP * per_box
    elements = particles * WINDOW * per_box
    return call(
        functools.partial(near_kernel, per_box=per_box, scale=(L_NEAR * per_box) ** (-0.5)),
        (near_rel, positions, there, feat, mix_t),
        [VMEM, VMEM],
        [
            jax.ShapeDtypeStruct((c, particles - 2 * EDGE * lanes), F32),
            jax.ShapeDtypeStruct((c, 2 * EDGE * lanes), F32),
        ],
        [pltpu.VMEM((WINDOW * per_box, lanes), BF)],
        "near_own",
        10,
        pl.CostEstimate(
            flops=2 * elements * c + 10 * elements,
            bytes_accessed=12 << 20,
            transcendentals=elements,
        ),
    )


def edge_weight_kernel(near_ref, here_ref, there_ref, out_ref, *, per_box, boxes):
    lanes = GROUP * per_box
    groups = boxes // GROUP
    for i in range(2 * EDGE):
        low = i < EDGE
        g = i if low else groups - 2 * EDGE + i
        at = pl.ds(g * lanes, lanes)
        counts = counts_of(near_ref[:, at], -HB if low else boxes)
        here = here_ref[:, at]
        for w in range(HB):
            there = there_ref[pl.ds((w if low else HB + w) * per_box, per_box), :]
            out_ref[i, pl.ds(w * per_box, per_box), :] = weights_of(here, there, counts[w : w + 1, :])


def edge_weights(near_rel, positions, there, boxes):
    per_box = positions.shape[1] // boxes
    lanes = GROUP * per_box
    return call(
        functools.partial(edge_weight_kernel, per_box=per_box, boxes=boxes),
        (near_rel, positions, there),
        VMEM,
        jax.ShapeDtypeStruct((2 * EDGE, HB * per_box, lanes), BF),
        [],
        "edge_weights",
        8,
    )


def near_edge_kernel(weight_ref, before_ref, after_ref, part_ref, mix_ref, out_ref, *, scale):
    lanes = weight_ref.shape[2]
    sums = []
    for i in range(2 * EDGE):
        source = (before_ref if i < EDGE else after_ref)[...]
        sums.append(part_ref[:, i * lanes : (i + 1) * lanes] + dot(source, weight_ref[i]))
    for i, total in enumerate(sums):
        out_ref[:, i * lanes : (i + 1) * lanes] = dot(mix_ref[...], (total * scale).astype(BF))


def near_edge(weights, before, after, part, mix_t, per_box):
    return call(
        functools.partial(near_edge_kernel, scale=(L_NEAR * per_box) ** (-0.5)),
        (weights, before, after, part, mix_t),
        VMEM,
        jax.ShapeDtypeStruct(part.shape, F32),
        [],
        "near_edge",
        8,
    )


def far_body(
    slot_hbm,
    class_hbm,
    ids_hbm,
    recv_hbm,
    trans_hbm,
    feat_hbm,
    basis_hbm,
    mid_hbm,
    edge_hbm,
    mix_hbm,
    out_hbm,
    send_ref,
    slot_ref,
    class_ref,
    pack_ref,
    recv_ref,
    trans_ref,
    feat_ref,
    basis_ref,
    mid_ref,
    edge_ref,
    mix_ref,
    out_ref,
    local_ref,
    in_sem,
    out_sem,
    ids_ref=None,
    mult_ref=None,
    stage_ref=None,
    send_sem=None,
    *,
    layer,
):
    k = basis_ref.shape[0]
    boxes = local_ref.shape[0] // k
    lanes = GROUP * out_ref.shape[1] // boxes
    groups = boxes // GROUP
    left = lax.broadcasted_iota(jnp.int32, (k, 2 * k), 1) < k
    sources = (slot_hbm, class_hbm, trans_hbm.at[layer], recv_hbm, basis_hbm, mid_hbm, feat_hbm, edge_hbm, mix_hbm.at[layer])
    targets = (slot_ref, class_ref, pack_ref, recv_ref, basis_ref, mid_ref, feat_ref, edge_ref, mix_ref)
    if ids_ref is not None:
        sources, targets = sources + (ids_hbm,), targets + (ids_ref,)
    copies = [pltpu.make_async_copy(x, y, in_sem.at[i]) for i, (x, y) in enumerate(zip(sources, targets))]
    for copy in copies:
        copy.start()

    def unpack(i):
        for j in range(UNPACK):
            pack = pack_ref[i * UNPACK + j]
            swap = jnp.concatenate([pack[:, k:], pack[:, :k]], axis=1)
            half = left[: k // 2]
            trans_ref[i * UNPACK + j] = jnp.concatenate(
                [jnp.where(half, pack, swap), jnp.where(half, swap, pack)], axis=0
            )

    def gather(s):
        for b in range(TARGETS):
            t = s * TARGETS + b
            total = None
            for first in range(0, L_FAR, TERMS):
                ids = [t * L_FAR + first + i for i in range(TERMS)]
                mats = [trans_ref[class_ref[i]] for i in ids]
                pairs = [jnp.where(left, mats[i], mats[i + 1]) for i in range(0, TERMS, 2)]
                blocks = jnp.concatenate([recv_ref[slot_ref[i]] for i in ids], axis=0)
                part = dot(jnp.concatenate(pairs, axis=1), blocks)
                total = part if total is None else total + part
            local_ref[pl.ds(pl.multiple_of(t * k, k), k), :] = (total * L_FAR ** (-0.5)).astype(BF)

    def tail(which, near):
        at = [pl.ds(pl.multiple_of(g * lanes, lanes), lanes) for g in which]
        rows = [pl.ds(pl.multiple_of(g * GROUP * k, GROUP * k), GROUP * k) for g in which]
        local = [local_ref[r, :] for r in rows]
        mixed = [dot_nt(mix_ref[...], x).astype(BF) for x in local]
        diag = [block_diagonal(basis_ref[:, a]) for a in at]
        update = [dot(m, d) * k ** (-0.5) + n[...] for m, d, n in zip(mixed, diag, near)]
        current = []
        for u, a in zip(update, at):
            silu = u * (0.5 + 0.5 * jnp.tanh(0.5 * u))
            current.append((feat_ref[:, a].astype(F32) + silu).astype(BF))
            out_ref[:, a] = current[-1]
        if mult_ref is not None:
            for g, d, x in zip(which, diag, current):
                store_multipole(mult_ref, g, d, x, (lanes // GROUP) ** (-0.5))

    copies[2].wait()
    pl.loop(0, pack_ref.shape[0] // UNPACK)(unpack)
    for i in (0, 1, 3):
        copies[i].wait()
    pl.loop(0, boxes // TARGETS)(gather)
    for copy in copies[4:]:
        copy.wait()
    stores = [
        pltpu.make_async_copy(
            out_ref.at[:, pl.ds(first * lanes, count * lanes)],
            out_hbm.at[:, pl.ds(first * lanes, count * lanes)],
            out_sem.at[i],
        )
        for i, (first, count) in enumerate(((EDGE, groups - 2 * EDGE), (0, EDGE), (groups - EDGE, EDGE)))
    ]

    def middle(s):
        inner = [s * BATCH + i for i in range(BATCH)]
        tail(
            [i + EDGE for i in inner],
            [mid_ref.at[:, pl.ds(pl.multiple_of(i * lanes, lanes), lanes)] for i in inner],
        )

    pl.loop(0, (groups - 2 * EDGE) // BATCH)(middle)
    stores[0].start()
    ends = list(range(EDGE)) + list(range(groups - EDGE, groups))
    tail(ends, [edge_ref.at[:, pl.ds(i * lanes, lanes)] for i in range(2 * EDGE)])
    for copy in stores[1:]:
        copy.start()
    if mult_ref is not None:
        send_all(ids_ref, mult_ref, stage_ref, send_ref, send_sem)
    for copy in stores:
        copy.wait()


def far_last_kernel(slot_hbm, class_hbm, *refs, layer):
    ins, out_ref, scratch = refs[:7], refs[7], refs[8:]
    far_body(slot_hbm, class_hbm, None, *ins, out_ref, None, *scratch, layer=layer)


def far_term(slots, classes, ids, tables, boxes, layer):
    recv, pack, feat, basis, mid, edge, mix = tables
    c, particles = feat.shape
    k = basis.shape[0]
    updated = jax.ShapeDtypeStruct((c, particles), BF)
    scratch = [
        pltpu.SMEM(slots.shape, jnp.int32),
        pltpu.SMEM(classes.shape, jnp.int32),
        pltpu.VMEM(pack.shape[1:], BF),
        pltpu.VMEM(recv.shape, BF),
        pltpu.VMEM((pack.shape[1], k, 2 * k), BF),
        pltpu.VMEM(feat.shape, BF),
        pltpu.VMEM(basis.shape, BF),
        pltpu.VMEM(mid.shape, F32),
        pltpu.VMEM(edge.shape, F32),
        pltpu.VMEM(mix.shape[1:], BF),
        pltpu.VMEM(feat.shape, BF),
        pltpu.VMEM((boxes * k, c), BF),
        pltpu.SemaphoreType.DMA((10,)),
        pltpu.SemaphoreType.DMA((3,)),
    ]
    if ids is None:
        kernel = functools.partial(far_last_kernel, layer=layer)
        return call(kernel, (slots, classes) + tables, ANY, updated, scratch, "far_last"), None
    n = ids.size
    scratch += [
        pltpu.SMEM(ids.shape, jnp.int32),
        pltpu.VMEM((boxes, k, c), BF),
        pltpu.VMEM((n, k, c), BF),
        pltpu.SemaphoreType.DMA((SENDS,)),
    ]
    return call(
        functools.partial(far_body, layer=layer),
        (slots, classes, ids) + tables,
        [ANY, ANY],
        [updated, jax.ShapeDtypeStruct((n, k, c), BF)],
        scratch,
        "far",
    )


def body(
    features,
    basis_values,
    positions,
    translation,
    far_mixing,
    near_mixing,
    send_box,
    source_dev,
    source_slot,
    offset_class,
    near_boxes,
):
    channels, particles = features.shape
    boxes = source_dev.shape[0]
    per_box = particles // boxes
    width = HB * per_box
    capacity = send_box.shape[2]
    ids = send_box[0].T
    slots = (place_of(source_dev) * capacity + source_slot).reshape(-1)
    classes = offset_class.reshape(-1)
    half = translation.shape[2] // 2
    trans = jnp.concatenate([translation[:, :, :half], translation[:, :, half:]], axis=-1)
    far_t = far_mixing.transpose(0, 2, 1)
    near_t = near_mixing.transpose(0, 2, 1)
    near_rel = (near_boxes - lax.axis_index(AXES) * boxes).T
    near_rel = jnp.repeat(near_rel, per_box, axis=1)
    near_rel = jnp.pad(near_rel, ((0, ROWS_NEAR - L_NEAR), (0, 0)), constant_values=-(1 << 20))
    current = features
    send = outgoing_blocks(ids, features, basis_values, boxes)
    there = positions.T
    for layer in range(LAYERS):
        received = exchange(send)
        before, after = halo(current, width)
        mid, part = near_own(near_rel, positions, there, current, near_t[layer], boxes)
        if layer == 0:
            ends = jnp.concatenate(halo(positions, width), axis=1).T
            weights = edge_weights(near_rel, positions, ends, boxes)
        edge = near_edge(weights, before, after, part, near_t[layer], per_box)
        tables = (received, trans, current, basis_values, mid, edge, far_t)
        current, send = far_term(slots, classes, None if layer == LAYERS - 1 else ids, tables, boxes, layer)
    return current


def solution(mesh):
    placed = (
        P(None, AXES),
        P(None, AXES),
        P(None, AXES),
        P(),
        P(),
        P(),
        P(AXES, None, None),
        P(AXES, None),
        P(AXES, None),
        P(AXES, None),
        P(AXES, None),
    )
    return jax.shard_map(body, mesh=mesh, in_specs=placed, out_specs=P(None, AXES), check_vma=False)
```
